1024 devices in a mesh: blk: 64 (over z_hi, x, y), grp: 16 (over z_lo, core).
Axes of the slice: x: 4, y: 4, z: 32 (z_hi: 4, z_lo: 8; z = z_hi * 8 + z_lo), core: 2. Of those that a mesh axis runs over, the one named last changes fastest.
Arguments:
- pooled_picture_vectors: bfloat16 [8192, 1536], P(('blk', 'grp')), may hold values from -6 to 6
- picture_mapping_matrix: bfloat16 [1536, 1152], replicated, may hold values from -0.15625 to 0.15625
- caption_vectors: bfloat16 [8192, 1152], P(('blk', 'grp')), may hold values from -6 to 6
- matching_caption_slot: int32 [8192], P(('blk', 'grp')), may hold values from 0 to 8191, each once
- picture_instance_class: int32 [8192], P(('blk', 'grp')), may hold values from 0 to 15
- caption_instance_class: int32 [8192], P(('blk', 'grp')), may hold values from 0 to 15
- score_scale: float32 [1], replicated, may hold values from 5 to 12
- score_offset: float32 [1], replicated, may hold values from -3 to -1
Outputs:
- image_grad: bfloat16 [8192, 1536], P(('blk', 'grp'))
- text_grad: bfloat16 [8192, 1152], P(('blk', 'grp'))
The draws below stay inside these ranges and needn't reach their ends.
Inputs may be any that keep to these rules, and one draw needn't show every extreme that they name: `matching_caption_slot`: every text is the positive of exactly one image.
All inputs are finite; a program needn't handle non-finite values.
Results may differ from the reference program's by a relative error of at most 0.028.
Values may be sent and summed in bfloat16 or wider, within the bound.
A program may use at most 32 MiB of HBM per device.

```python
import jax
import jax.numpy as jnp
from jax import lax

D = 1152
FEATS = 1536
GROUPS = 16
ROWS_DEV = 8
BATCH = 8192
N_GRP = 16


def set_ends(entries, stream_key, low, largest):
    index_at = [jax.random.randint(jax.random.fold_in(stream_key, axis), (), 0, length) for axis, length in enumerate(entries.shape)]
    widest = entries.shape.index(max(entries.shape))
    neighbour = index_at[:widest] + [(index_at[widest] + 1) % entries.shape[widest]] + index_at[widest + 1:]
    return entries.at[tuple(index_at)].set(low).at[tuple(neighbour)].set(largest)


def levels(rng, shape, shards, least, largest):
    def one(position, blocks):
        steps = jax.random.uniform(jax.random.fold_in(jax.random.fold_in(rng, 6), position), (blocks,), jnp.float32, least / len(shards), largest / len(shards))
        return jnp.repeat(jnp.exp(steps), shape[position] // blocks).reshape((-1,) + (1,) * (len(shape) - position - 1))

    gain = one(*shards[0])
    for cut in shards[1:]:
        gain = gain * one(*cut)
    return gain


def normal_values(key, dims, scale, most, shards=(), kind=jnp.bfloat16):
    gain = levels(key, dims, shards, -0.22, 0.18) if shards else 1.0
    entries = jax.random.normal(key, dims, jnp.float32) * scale * gain
    return jnp.minimum(jnp.maximum(entries, -most), most).astype(kind)


def setup_inputs(seed: int = 0) -> dict:
    arg_keys = jax.random.split(jax.random.key(seed), 9)
    return {
        "pooled_picture_vectors": normal_values(arg_keys[0], (BATCH, FEATS), 1.0, 6.0, ((0, 1024),)),
        "picture_mapping_matrix": normal_values(arg_keys[1], (FEATS, D), FEATS ** -0.5, 0.15625),
        "caption_vectors": normal_values(arg_keys[2], (BATCH, D), 1.0, 6.0, ((0, 1024),)),
        "matching_caption_slot": jax.random.permutation(arg_keys[3], BATCH).astype(jnp.int32),
        "picture_instance_class": set_ends(jax.random.randint(arg_keys[4], (BATCH,), 0, GROUPS), jax.random.fold_in(arg_keys[4], 1), 0, GROUPS - 1).astype(jnp.int32),
        "caption_instance_class": set_ends(jax.random.randint(arg_keys[5], (BATCH,), 0, GROUPS), jax.random.fold_in(arg_keys[5], 1), 0, GROUPS - 1).astype(jnp.int32),
        "score_scale": jnp.clip(jax.random.uniform(arg_keys[6], (1,), jnp.float32, 5.0, 12.0), 5.0, 12.0),
        "score_offset": jnp.clip(jax.random.uniform(arg_keys[7], (1,), jnp.float32, -3.0, -1.0), -3.0, -1.0),
    }


epsilon = 1e-06

def normalize(values):
    norm_rows = jnp.sqrt(lax.optimization_barrier(jnp.sum(values * values, axis=1, keepdims=True)) + epsilon)
    return (values / norm_rows, norm_rows)

def reference(pooled_picture_vectors, picture_mapping_matrix, caption_vectors, matching_caption_slot, picture_instance_class, caption_instance_class, score_scale, score_offset):
    embedded = jnp.dot(pooled_picture_vectors, picture_mapping_matrix, preferred_element_type=jnp.float32)
    image_dir, image_norm = normalize(embedded)
    image_unit = image_dir.astype(jnp.bfloat16)
    text_dir, text_norm = normalize(caption_vectors.astype(jnp.float32))
    caption_direction = text_dir.astype(jnp.bfloat16)
    block_rows = ROWS_DEV * N_GRP
    block_count = BATCH // block_rows
    text_index = jnp.arange(BATCH, dtype=jnp.int32)
    scaled_score_factor = score_scale[0]
    offset_amount = score_offset[0]

    def visit(text_acc, inputs):
        normalized_vectors, pair_rows, group_rows = inputs
        similarity_scores = jnp.dot(normalized_vectors, caption_direction.T, preferred_element_type=jnp.float32) * scaled_score_factor + offset_amount
        positive = pair_rows[:, None] == text_index[None, :]
        match_sign = jnp.where(positive, 1.0, -1.0).astype(jnp.float32)
        same = group_rows[:, None] == caption_instance_class[None, :]
        retained_match_mask = jnp.where(same & jnp.logical_not(positive), 0.0, 1.0).astype(jnp.float32)
        loss_weight_factor = (-retained_match_mask * match_sign * jax.nn.sigmoid(-match_sign * similarity_scores) * scaled_score_factor).astype(jnp.bfloat16)
        image_part = jnp.dot(loss_weight_factor, caption_direction, preferred_element_type=jnp.float32)
        text_acc = text_acc + jnp.dot(loss_weight_factor.T, normalized_vectors, preferred_element_type=jnp.float32)
        return (text_acc, image_part)
    stacked = (image_unit.reshape(block_count, block_rows, D), matching_caption_slot.reshape(block_count, block_rows), picture_instance_class.reshape(block_count, block_rows))
    text_unit_grad, image_parts = lax.scan(visit, jnp.zeros((BATCH, D), jnp.float32), stacked)
    image_unit_grad = image_parts.reshape(BATCH, D)
    inner = lax.optimization_barrier(jnp.sum(image_dir * image_unit_grad, axis=1, keepdims=True))
    embed_grad = ((image_unit_grad - image_dir * inner) / image_norm).astype(jnp.bfloat16)
    image_grad = jnp.dot(embed_grad, picture_mapping_matrix.T, preferred_element_type=jnp.float32).astype(jnp.bfloat16)
    text_inner = lax.optimization_barrier(jnp.sum(text_dir * text_unit_grad, axis=1, keepdims=True))
    text_grad = ((text_unit_grad - text_dir * text_inner) / text_norm).astype(jnp.bfloat16)
    return (image_grad, text_grad)
```

```python
import jax
import jax.numpy as jnp
from jax import lax
from jax.experimental import pallas as pl
from jax.experimental.pallas import tpu as pltpu
from jax.sharding import PartitionSpec as P

epsilon = 1e-06
D = 1152
FEATS = 1536
ROWS = 8
TILES = D // 128
FOLD = (TILES + 1) * ROWS
MESH = pl.DeviceIdType.MESH

IMAGE_Z = tuple(range(-4, 4))
TEXT_Z = (-12, -4, 4, 12)
IMAGE_XY = ((0, 0), (1, 0), (0, 1), (1, 1))
TEXT_XY = ((1, 1), (1, -1), (-1, 1), (-1, -1))
OWN_Z = IMAGE_Z.index(0)


def fold(rows):
    pieces = [rows[:, 128 * t : 128 * (t + 1)] for t in range(TILES)]
    pieces.append(jnp.zeros((ROWS, 128), jnp.float32))
    return jnp.concatenate(pieces, axis=0).astype(jnp.bfloat16)


def unfold(block):
    return jnp.concatenate([block[ROWS * t : ROWS * (t + 1)] for t in range(TILES)], axis=1)


def normalize(values):
    norm_rows = jnp.sqrt(jnp.sum(values * values, axis=1, keepdims=True) + epsilon)
    return values / norm_rows, norm_rows


def column(ref, row, shift, mask):
    out = jnp.zeros((ROWS, 128), jnp.int32)
    for r in range(ROWS):
        out = jnp.where(row == r, lax.bitwise_and(lax.shift_right_logical(ref[r], shift), mask), out)
    return out


def kernel(
    scale_ref, offset_ref, slot_ref, iclass_ref, tclass_ref, pooled_ref, caption_ref, w_hbm,
    image_out, text_out,
    w_ref, img, ztxt, txt, x_ref, y_ref, mx_ref, my_ref,
    ig_ref, tg_ref, s_out, s_in, p_txt, p_txt_in, p_img, p_img_in, z_txt, z_txt_in, z_img, z_img_in, o_txt,
    w_sem, send, recv,
):
    blk = lax.axis_index("blk")
    grp = lax.axis_index("grp")
    x, y, z, core = (blk // 4) % 4, blk % 4, (blk // 16) * 8 + grp // 2, grp % 2
    sign = 1 - 2 * core

    def device(dx=0, dy=0, dz=0, other=False):
        to_x, to_y, to_z = (x + dx + 4) % 4, (y + dy + 4) % 4, (z + dz + 32) % 32
        to_core = 1 - core if other else core
        return ((to_z // 8) * 16 + to_x * 4 + to_y, (to_z % 8) * 2 + to_core)

    partners = [dict(other=True)]
    partners += [dict(dz=d) for d in (-12, 12, -4, 4, -3, 3, -2, 2, -1, 1)]
    partners += [dict(dx=dx, dy=dy) for dx in (-1, 0, 1) for dy in (-1, 0, 1) if dx or dy]
    barrier = pltpu.get_barrier_semaphore()
    for p in partners:
        pl.semaphore_signal(barrier, inc=1, device_id=device(**p), device_id_type=MESH)

    w_copy = pltpu.make_async_copy(w_hbm, w_ref, w_sem)
    w_copy.start()

    row = lax.broadcasted_iota(jnp.int32, (ROWS, 128), 0)
    lane = lax.broadcasted_iota(jnp.int32, (ROWS, 128), 1)

    text_dir, text_norm = normalize(caption_ref[...].astype(jnp.float32))
    text_label = jnp.where(lane == 0, column(tclass_ref, row, 0, 15), jnp.where(lane == 1, blk, grp * ROWS + row))
    own_text = jnp.concatenate(
        [text_dir[:, 128 * t : 128 * (t + 1)] for t in range(TILES)] + [text_label.astype(jnp.float32)], axis=0
    )
    s_out[0] = own_text.astype(jnp.bfloat16)

    w_copy.wait()
    embedded = jnp.dot(pooled_ref[...], w_ref[...], preferred_element_type=jnp.float32)
    image_dir, image_norm = normalize(embedded)
    image_label = jnp.where(
        lane == 0, column(iclass_ref, row, 0, 15),
        jnp.where(lane == 1, column(slot_ref, row, 7, 63), column(slot_ref, row, 0, 127)),
    )
    own_image = jnp.concatenate(
        [image_dir[:, 128 * t : 128 * (t + 1)] for t in range(TILES)] + [image_label.astype(jnp.float32)], axis=0
    )
    img[0, OWN_Z] = own_image.astype(jnp.bfloat16)

    pl.semaphore_wait(barrier, len(partners))

    count = [0]

    def copy(src, dst, **to):
        n = count[0]
        count[0] += 1
        c = pltpu.make_async_remote_copy(
            src_ref=src, dst_ref=dst, send_sem=send.at[n], recv_sem=recv.at[n],
            device_id=device(**to), device_id_type=MESH,
        )
        c.start()
        return c

    def arrive(copies):
        for c in copies:
            c.wait_recv()

    started = []
    stage_t = [copy(s_out.at[0], ztxt.at[n], dz=-b) for n, b in enumerate(TEXT_Z)]
    stage_i = [
        copy(img.at[0, OWN_Z], img.at[0, n], dz=-sign * k) for n, k in enumerate(IMAGE_Z) if k
    ]
    started += stage_t + stage_i
    arrive(stage_i)
    plane_i = [
        copy(img.at[0], img.at[q], dx=-sign * ax, dy=-sign * ay) for q, (ax, ay) in enumerate(IMAGE_XY) if q
    ]
    arrive(stage_t)
    plane_t = [copy(ztxt, txt.at[0, q], dx=-bx, dy=-by) for q, (bx, by) in enumerate(TEXT_XY)]
    started += plane_i + plane_t
    arrive(plane_t)
    across = copy(txt.at[0], txt.at[1], other=True)
    started.append(across)

    def spread(block_of, dst, label, n):
        a, b = block_of(2 * n).astype(jnp.float32), block_of(2 * n + 1).astype(jnp.float32)
        at = pl.ds(pl.multiple_of(16 * n, 16), 16)
        dst[at, :] = jnp.concatenate([unfold(a), unfold(b)], axis=0).astype(jnp.bfloat16)
        label[at, :] = jnp.concatenate([a[ROWS * TILES :], b[ROWS * TILES :]], axis=0).astype(jnp.bfloat16)

    arrive(plane_i)
    for n in range(16):
        spread(lambda j: img[j // 8, j % 8], x_ref, mx_ref, n)
    for n in range(8):
        spread(lambda j: txt[0, j // 4, j % 4], y_ref, my_ref, n)
    arrive([across])
    for n in range(8, 16):
        spread(lambda j: txt[1, (j - 16) // 4, j % 4], y_ref, my_ref, n)

    scale, offset = scale_ref[0], offset_ref[0]
    nt = (((1,), (1,)), ((), ()))
    scores = lax.dot_general(x_ref[...], y_ref[...], nt, preferred_element_type=jnp.float32) * scale + offset
    pick_row = lax.broadcasted_iota(jnp.int32, (ROWS, 128), 0)
    basis = jnp.where(
        pick_row == 0, jnp.where(lane == 0, 1.0, 0.0),
        jnp.where(pick_row == 1, jnp.where(lane == 1, 128.0, jnp.where(lane == 2, 1.0, 0.0)), 0.0),
    ).astype(jnp.bfloat16)
    text_rows = lax.dot_general(basis, my_ref[...], nt, preferred_element_type=jnp.float32)
    image_columns = lax.dot_general(mx_ref[...], basis, nt, preferred_element_type=jnp.float32)
    positive = image_columns[:, 1:2] == text_rows[1:2, :]
    same = image_columns[:, 0:1] == text_rows[0:1, :]
    sigmoid = 1.0 / (1.0 + jnp.exp(jnp.where(positive, scores, -scores)))
    signed = jnp.where(positive, -scale, jnp.where(same, 0.0, scale))
    weight = (sigmoid * signed).astype(jnp.bfloat16)

    tg_ref[...] = lax.dot_general(
        weight, x_ref[...], (((0,), (0,)), ((), ())), preferred_element_type=jnp.float32
    )
    for n in range(16):
        s_in[n] = fold(tg_ref[128 + 8 * n : 136 + 8 * n, :])
    back_across = copy(s_in, p_txt, other=True)
    ig_ref[...] = jnp.dot(weight, y_ref[...], preferred_element_type=jnp.float32)
    for n in range(32):
        p_img[n // 8, n % 8] = fold(ig_ref[8 * n : 8 * n + 8, :])
    back_i = [
        copy(p_img.at[q], p_img_in.at[q], dx=sign * ax, dy=sign * ay) for q, (ax, ay) in enumerate(IMAGE_XY) if q
    ]
    arrive([back_across])
    for n in range(16):
        mine = fold(tg_ref[8 * n : 8 * n + 8, :]).astype(jnp.float32)
        z_txt[n] = (mine + p_txt[n].astype(jnp.float32)).astype(jnp.bfloat16)
    back_t = [copy(z_txt.at[pl.ds(4 * q, 4)], p_txt_in.at[q], dx=bx, dy=by) for q, (bx, by) in enumerate(TEXT_XY)]
    started += [back_across] + back_i + back_t

    arrive(back_i)
    home_i = []
    for n, k in enumerate(IMAGE_Z):
        total = p_img[0, n].astype(jnp.float32)
        for q in range(1, 4):
            total += p_img_in[q, n].astype(jnp.float32)
        z_img[n] = total.astype(jnp.bfloat16)
        if k:
            home_i.append(copy(z_img.at[n], z_img_in.at[n], dz=sign * k))
    arrive(back_t)
    home_t = []
    for n, b in enumerate(TEXT_Z):
        total = p_txt_in[0, n].astype(jnp.float32)
        for q in range(1, 4):
            total += p_txt_in[q, n].astype(jnp.float32)
        o_txt[n] = total.astype(jnp.bfloat16)
        home_t.append(copy(o_txt.at[n], z_txt_in.at[n], dz=b))
    started += home_i + home_t

    arrive(home_i)
    total = z_img[OWN_Z].astype(jnp.float32)
    for n, k in enumerate(IMAGE_Z):
        if k:
            total += z_img_in[n].astype(jnp.float32)
    grad = unfold(total)
    inner = jnp.sum(image_dir * grad, axis=1, keepdims=True)
    embed_grad = ((grad - image_dir * inner) / image_norm).astype(jnp.bfloat16)
    image_out[...] = lax.dot_general(embed_grad, w_ref[...], nt, preferred_element_type=jnp.float32).astype(
        jnp.bfloat16
    )
    arrive(home_t)
    total = z_txt_in[0].astype(jnp.float32)
    for n in range(1, 4):
        total += z_txt_in[n].astype(jnp.float32)
    grad = unfold(total)
    inner = jnp.sum(text_dir * grad, axis=1, keepdims=True)
    text_out[...] = ((grad - text_dir * inner) / text_norm).astype(jnp.bfloat16)
    for c in started:
        c.wait_send()


def body(
    pooled_picture_vectors,
    picture_mapping_matrix,
    caption_vectors,
    matching_caption_slot,
    picture_instance_class,
    caption_instance_class,
    score_scale,
    score_offset,
):
    smem = pl.BlockSpec(memory_space=pltpu.SMEM)
    vmem = pl.BlockSpec(memory_space=pltpu.VMEM)
    half = jnp.bfloat16
    return pl.pallas_call(
        kernel,
        out_shape=(
            jax.ShapeDtypeStruct((ROWS, FEATS), half),
            jax.ShapeDtypeStruct((ROWS, D), half),
        ),
        in_specs=[smem] * 5 + [vmem] * 2 + [pl.BlockSpec(memory_space=pl.ANY)],
        out_specs=(vmem, vmem),
        scratch_shapes=[
            pltpu.VMEM((FEATS, D), half),
            pltpu.VMEM((4, 8, FOLD, 128), half),
            pltpu.VMEM((4, FOLD, 128), half),
            pltpu.VMEM((2, 4, 4, FOLD, 128), half),
            pltpu.VMEM((256, D), half),
            pltpu.VMEM((256, D), half),
            pltpu.VMEM((256, 128), half),
            pltpu.VMEM((256, 128), half),
            pltpu.VMEM((256, D), jnp.float32),
            pltpu.VMEM((256, D), jnp.float32),
            pltpu.VMEM((1, FOLD, 128), half),
            pltpu.VMEM((16, FOLD, 128), half),
            pltpu.VMEM((16, FOLD, 128), half),
            pltpu.VMEM((4, 4, FOLD, 128), half),
            pltpu.VMEM((4, 8, FOLD, 128), half),
            pltpu.VMEM((4, 8, FOLD, 128), half),
            pltpu.VMEM((16, FOLD, 128), half),
            pltpu.VMEM((4, FOLD, 128), half),
            pltpu.VMEM((8, FOLD, 128), half),
            pltpu.VMEM((8, FOLD, 128), half),
            pltpu.VMEM((4, FOLD, 128), half),
            pltpu.SemaphoreType.DMA,
            pltpu.SemaphoreType.DMA((40,)),
            pltpu.SemaphoreType.DMA((40,)),
        ],
        compiler_params=pltpu.CompilerParams(
            collective_id=0, has_side_effects=True, vmem_limit_bytes=40 * 2**20
        ),
        name="contrast",
    )(
        score_scale, score_offset, matching_caption_slot, picture_instance_class, caption_instance_class,
        pooled_picture_vectors, caption_vectors, picture_mapping_matrix,
    )


def solution(mesh):
    placed = (
        P(("blk", "grp"), None),
        P(),
        P(("blk", "grp"), None),
        P(("blk", "grp")),
        P(("blk", "grp")),
        P(("blk", "grp")),
        P(),
        P(),
    )
    return jax.shard_map(
        body,
        mesh=mesh,
        in_specs=placed,
        out_specs=(P(("blk", "grp"), None), P(("blk", "grp"), None)),
        check_vma=False,
    )
```

```python
import jax
import jax.numpy as jnp
from jax import lax
from jax.experimental import pallas as pl
from jax.experimental.pallas import tpu as pltpu
from jax.sharding import PartitionSpec as P

epsilon = 1e-06
D = 1152
FEATS = 1536
ROWS = 8
TILES = D // 128
FOLD = (TILES + 1) * ROWS
MESH = pl.DeviceIdType.MESH

IMAGE_Z = ((0, -1), (1, -2), (2, -3), (3, -4))
TEXT_Z = ((-4, 4), (-12, 12))
IMAGE_XY = ((0, 0), (1, 0), (0, 1), (1, 1))
TEXT_XY = ((1, 1), (1, -1), (-1, 1), (-1, -1))
CHUNKS = 3
NT = (((1,), (1,)), ((), ()))
TN = (((0,), (0,)), ((), ()))


def fold(rows):
    pieces = [rows[:, 128 * t : 128 * (t + 1)] for t in range(TILES)]
    pieces.append(jnp.zeros((ROWS, 128), jnp.float32))
    return jnp.concatenate(pieces, axis=0).astype(jnp.bfloat16)


def unfold(block):
    return jnp.concatenate([block[ROWS * t : ROWS * (t + 1)] for t in range(TILES)], axis=1)


def normalize(values):
    norm_rows = jnp.sqrt(jnp.sum(values * values, axis=1, keepdims=True) + epsilon)
    return values / norm_rows, norm_rows


def column(ref, row, shift, mask):
    out = jnp.zeros((ROWS, 128), jnp.int32)
    for r in range(ROWS):
        out = jnp.where(row == r, lax.bitwise_and(lax.shift_right_logical(ref[r], shift), mask), out)
    return out


def kernel(
    scale_ref, offset_ref, slot_hbm, iclass_hbm, tclass_hbm, pooled_hbm, caption_hbm, w_hbm,
    image_out, text_out,
    slot_ref, iclass_ref, tclass_ref, pooled_ref, caption_ref, w_ref, wt_ref,
    own_text, img, ztxt, via, txt, x_ref, y_ref, mx_ref, my_ref, tg_ref, ig_ref,
    r0, r0_in, rt1, rt1_in, rt2, rt2_in, ri1, ri1_in, ri2, ri2_in,
    load, send, recv,
):
    blk = lax.axis_index("blk")
    grp = lax.axis_index("grp")
    x, y, z, core = (blk // 4) % 4, blk % 4, (blk // 16) * 8 + grp // 2, grp % 2
    sign = 1 - 2 * core

    def device(dx=0, dy=0, dz=0, other=False):
        to_x, to_y, to_z = (x + dx + 4) % 4, (y + dy + 4) % 4, (z + dz + 32) % 32
        to_core = 1 - core if other else core
        return ((to_z // 8) * 16 + to_x * 4 + to_y, (to_z % 8) * 2 + to_core)

    rows_w = FEATS // CHUNKS
    loads = [
        pltpu.make_async_copy(src, dst, load.at[n])
        for n, (src, dst) in enumerate(
            [(caption_hbm, caption_ref), (tclass_hbm, tclass_ref), (pooled_hbm, pooled_ref)]
            + [(w_hbm.at[pl.ds(rows_w * n, rows_w)], w_ref.at[pl.ds(rows_w * n, rows_w)]) for n in range(CHUNKS)]
            + [(iclass_hbm, iclass_ref), (slot_hbm, slot_ref)]
        )
    ]
    for c in loads:
        c.start()
    partners = [dict(dz=d) for d in (-4, 4, -3, 3, -2, 2, -1, 1)]
    partners += [dict(dx=dx, dy=dy) for dx in (-1, 0, 1) for dy in (-1, 0, 1) if dx or dy]
    partners += [dict(other=True)]
    barrier = pltpu.get_barrier_semaphore()
    for p in partners:
        pl.semaphore_signal(barrier, inc=1, device_id=device(**p), device_id_type=MESH)

    row = lax.broadcasted_iota(jnp.int32, (ROWS, 128), 0)
    lane = lax.broadcasted_iota(jnp.int32, (ROWS, 128), 1)

    def block_of(values, label):
        pieces = [values[:, 128 * t : 128 * (t + 1)] for t in range(TILES)]
        return jnp.concatenate(pieces + [label.astype(jnp.float32)], axis=0).astype(jnp.bfloat16)

    loads[0].wait()
    loads[1].wait()
    text_dir, text_norm = normalize(caption_ref[...].astype(jnp.float32))
    label = jnp.where(lane == 0, column(tclass_ref, row, 0, 15), jnp.where(lane == 1, blk, grp * ROWS + row))
    own_text[...] = block_of(text_dir, label)
    loads[2].wait()
    embedded = jnp.zeros((ROWS, D), jnp.float32)
    for n in range(CHUNKS):
        loads[3 + n].wait()
        at = slice(rows_w * n, rows_w * (n + 1))
        embedded += jnp.dot(pooled_ref[:, at], w_ref[at, :], preferred_element_type=jnp.float32)
    image_dir, image_norm = normalize(embedded)
    loads[-2].wait()
    loads[-1].wait()
    label = jnp.where(
        lane == 0, column(iclass_ref, row, 0, 15),
        jnp.where(lane == 1, column(slot_ref, row, 7, 63), column(slot_ref, row, 0, 127)),
    )
    img[0, 0, 0] = block_of(image_dir, label)

    pl.semaphore_wait(barrier, len(partners))

    started = []

    def copy(src, dst, **to):
        n = copy.count
        copy.count += 1
        c = pltpu.make_async_remote_copy(
            src_ref=src, dst_ref=dst, send_sem=send.at[n], recv_sem=recv.at[n],
            device_id=device(**to), device_id_type=MESH,
        )
        c.start()
        started.append(c)
        return c

    copy.count = 0

    def drain():
        while started:
            started.pop(0).wait_send()

    near = [copy(own_text, ztxt.at[0, i], dz=-b) for i, b in enumerate(TEXT_Z[0])]
    along = {}
    for p in (3, 2, 1, 0):
        for i in (1, 0):
            k = IMAGE_Z[p][i]
            if k:
                along[p, i] = copy(img.at[0, 0, 0], img.at[0, p, i], dz=-sign * k)

    plane_i = {}

    def forward_image(p):
        for i in (0, 1):
            if IMAGE_Z[p][i]:
                along[p, i].wait_recv()
        for q in (3, 2, 1):
            ax, ay = IMAGE_XY[q]
            plane_i[p, q] = copy(img.at[0, p], img.at[q, p], dx=-sign * ax, dy=-sign * ay)

    def forward_text(p):
        return [copy(ztxt.at[p], txt.at[p, 0, q], dx=-bx, dy=-by) for q, (bx, by) in enumerate(TEXT_XY)]

    def spread(pair, dst, label, n):
        a, b = pair[0].astype(jnp.float32), pair[1].astype(jnp.float32)
        at = slice(16 * n, 16 * n + 16)
        dst[at, :] = jnp.concatenate([unfold(a), unfold(b)], axis=0).astype(jnp.bfloat16)
        label[at, :] = jnp.concatenate([a[ROWS * TILES :], b[ROWS * TILES :]], axis=0).astype(jnp.bfloat16)

    def spread_image(p, q):
        if q:
            plane_i[p, q].wait_recv()
        spread(img.at[q, p], x_ref, mx_ref, 4 * q + p)

    def spread_text(p, h, q):
        spread(txt.at[p, h, q], y_ref, my_ref, 8 * p + 4 * h + q)

    forward_image(0)
    forward_image(1)
    forward_image(2)
    for c in near:
        c.wait_recv()
    middle = [copy(ztxt.at[0, i], via.at[i], dz=-b) for i, b in enumerate(TEXT_Z[0])]
    plane_t = forward_text(0)
    forward_image(3)
    for p in range(4):
        spread_image(p, 0)
    for p in range(3):
        for q in (1, 2, 3):
            spread_image(p, q)

    def cross_text(p, plane):
        across = []
        for q in range(4):
            plane[q].wait_recv()
            across.append(copy(txt.at[p, 0, q], txt.at[p, 1, q], other=True))
        return across

    across = cross_text(0, plane_t)
    for q in (1, 2, 3):
        spread_image(3, q)
    for c in middle:
        c.wait_recv()
    far = [copy(via.at[i], ztxt.at[1, i], dz=-b) for i, b in enumerate(TEXT_Z[0])]

    scale, offset = scale_ref[0], offset_ref[0]
    basis = jnp.where(
        row == 0, jnp.where(lane == 0, 1.0, 0.0),
        jnp.where(row == 1, jnp.where(lane == 1, 128.0, jnp.where(lane == 2, 1.0, 0.0)), 0.0),
    ).astype(jnp.bfloat16)
    image_columns = lax.dot_general(mx_ref[...], basis, NT, preferred_element_type=jnp.float32)

    def weigh(p):
        at = slice(128 * p, 128 * p + 128)
        scores = lax.dot_general(x_ref[...], y_ref[at, :], NT, preferred_element_type=jnp.float32) * scale + offset
        text_rows = lax.dot_general(basis, my_ref[at, :], NT, preferred_element_type=jnp.float32)
        positive = image_columns[:, 1:2] == text_rows[1:2, :]
        same = image_columns[:, 0:1] == text_rows[0:1, :]
        sigmoid = 1.0 / (1.0 + jnp.exp(jnp.where(positive, scores, -scores)))
        signed = jnp.where(positive, -scale, jnp.where(same, 0.0, scale))
        weight = (sigmoid * signed).astype(jnp.bfloat16)
        tg_ref[at, :] = lax.dot_general(weight, x_ref[...], TN, preferred_element_type=jnp.float32)
        for n in range(8):
            r0[p, n] = fold(tg_ref[128 * p + 64 + 8 * n : 128 * p + 72 + 8 * n, :])
        return weight, copy(r0.at[p], r0_in.at[p], other=True)

    def back_text(p, crossed):
        crossed.wait_recv()
        out = []
        for q, (bx, by) in enumerate(TEXT_XY):
            for i in (0, 1):
                n = 2 * q + i
                mine = tg_ref[128 * p + 8 * n : 128 * p + 8 * n + 8, :]
                rt1[p, q, i] = fold(mine + unfold(r0_in[p, n].astype(jnp.float32)))
            out.append(copy(rt1.at[p, q], rt1_in.at[p, q], dx=bx, dy=by))
        return out

    def home_text(p, arriving):
        for c in arriving:
            c.wait_recv()
        out = []
        for i, b in enumerate(TEXT_Z[p]):
            total = rt1_in[p, 0, i].astype(jnp.float32)
            for q in (1, 2, 3):
                total += rt1_in[p, q, i].astype(jnp.float32)
            rt2[p, i] = total.astype(jnp.bfloat16)
            out.append(copy(rt2.at[p, i], rt2_in.at[p, i], dz=b))
        return out

    for q in range(4):
        spread_text(0, 0, q)
    for q in range(4):
        across[q].wait_recv()
        spread_text(0, 1, q)
    weight, crossed = weigh(0)
    ig_ref[...] = jnp.dot(weight, y_ref[0:128, :], preferred_element_type=jnp.float32)
    returning = back_text(0, crossed)

    for c in far:
        c.wait_recv()
    plane_t = forward_text(1)
    home_t = home_text(0, returning)
    for n in range(FEATS // 128):
        at = slice(128 * n, 128 * n + 128)
        wt_ref[:, at] = w_ref[at, :].T
    across = cross_text(1, plane_t)
    for q in range(4):
        spread_text(1, 0, q)
    for q in range(4):
        across[q].wait_recv()
        spread_text(1, 1, q)
    weight, crossed = weigh(1)
    ig_ref[...] += jnp.dot(weight, y_ref[128:256, :], preferred_element_type=jnp.float32)
    back_i = {}
    for p in (3, 2, 1, 0):
        for q in (3, 2, 1, 0):
            ax, ay = IMAGE_XY[q]
            for i in (0, 1):
                n = 8 * q + 2 * p + i
                ri1[q, p, i] = fold(ig_ref[8 * n : 8 * n + 8, :])
            if q:
                back_i[p, q] = copy(ri1.at[q, p], ri1_in.at[q, p], dx=sign * ax, dy=sign * ay)
        if p == 3:
            returning = back_text(1, crossed)

    home_i = []

    def home_image(p):
        for q in (3, 2, 1):
            back_i[p, q].wait_recv()
        for i in (1, 0):
            total = ri1[0, p, i].astype(jnp.float32)
            for q in (1, 2, 3):
                total += ri1_in[q, p, i].astype(jnp.float32)
            ri2[p, i] = total.astype(jnp.bfloat16)
            if IMAGE_Z[p][i]:
                home_i.append(copy(ri2.at[p, i], ri2_in.at[p, i], dz=sign * IMAGE_Z[p][i]))

    home_image(3)
    home_t += home_text(1, returning)
    home_image(2)
    home_image(1)
    home_image(0)
    drain()

    for c in home_i:
        c.wait_recv()
    total = ri2[0, 0].astype(jnp.float32)
    for p in range(4):
        for i in (0, 1):
            if IMAGE_Z[p][i]:
                total += ri2_in[p, i].astype(jnp.float32)
    grad = unfold(total)
    inner = jnp.sum(image_dir * grad, axis=1, keepdims=True)
    embed_grad = ((grad - image_dir * inner) / image_norm).astype(jnp.bfloat16)
    image_out[...] = jnp.dot(embed_grad, wt_ref[...], preferred_element_type=jnp.float32).astype(jnp.bfloat16)
    for c in home_t:
        c.wait_recv()
    total = rt2_in[0, 0].astype(jnp.float32)
    for p, i in ((0, 1), (1, 0), (1, 1)):
        total += rt2_in[p, i].astype(jnp.float32)
    grad = unfold(total)
    inner = jnp.sum(text_dir * grad, axis=1, keepdims=True)
    text_out[...] = ((grad - text_dir * inner) / text_norm).astype(jnp.bfloat16)


def body(
    pooled_picture_vectors,
    picture_mapping_matrix,
    caption_vectors,
    matching_caption_slot,
    picture_instance_class,
    caption_instance_class,
    score_scale,
    score_offset,
):
    smem = pl.BlockSpec(memory_space=pltpu.SMEM)
    vmem = pl.BlockSpec(memory_space=pltpu.VMEM)
    hbm = pl.BlockSpec(memory_space=pltpu.HBM)
    half = jnp.bfloat16
    block = (FOLD, 128)
    return pl.pallas_call(
        kernel,
        out_shape=(
            jax.ShapeDtypeStruct((ROWS, FEATS), half),
            jax.ShapeDtypeStruct((ROWS, D), half),
        ),
        in_specs=[smem] * 2 + [hbm] * 6,
        out_specs=(vmem, vmem),
        scratch_shapes=[
            pltpu.SMEM((ROWS,), jnp.int32),
            pltpu.SMEM((ROWS,), jnp.int32),
            pltpu.SMEM((ROWS,), jnp.int32),
            pltpu.VMEM((ROWS, FEATS), half),
            pltpu.VMEM((ROWS, D), half),
            pltpu.VMEM((FEATS, D), half),
            pltpu.VMEM((D, FEATS), half),
            pltpu.VMEM(block, half),
            pltpu.VMEM((4, 4, 2) + block, half),
            pltpu.VMEM((2, 2) + block, half),
            pltpu.VMEM((2,) + block, half),
            pltpu.VMEM((2, 2, 4, 2) + block, half),
            pltpu.VMEM((256, D), half),
            pltpu.VMEM((256, D), half),
            pltpu.VMEM((256, 128), half),
            pltpu.VMEM((256, 128), half),
            pltpu.VMEM((256, D), jnp.float32),
            pltpu.VMEM((256, D), jnp.float32),
            pltpu.VMEM((2, 8) + block, half),
            pltpu.VMEM((2, 8) + block, half),
            pltpu.VMEM((2, 4, 2) + block, half),
            pltpu.VMEM((2, 4, 2) + block, half),
            pltpu.VMEM((2, 2) + block, half),
            pltpu.VMEM((2, 2) + block, half),
            pltpu.VMEM((4, 4, 2) + block, half),
            pltpu.VMEM((4, 4, 2) + block, half),
            pltpu.VMEM((4, 2) + block, half),
            pltpu.VMEM((4, 2) + block, half),
            pltpu.SemaphoreType.DMA((8,)),
            pltpu.SemaphoreType.DMA((80,)),
            pltpu.SemaphoreType.DMA((80,)),
        ],
        compiler_params=pltpu.CompilerParams(
            collective_id=0, has_side_effects=True, vmem_limit_bytes=60 * 2**20
        ),
        name="contrast",
    )(
        score_scale, score_offset, matching_caption_slot, picture_instance_class, caption_instance_class,
        pooled_picture_vectors, caption_vectors, picture_mapping_matrix,
    )


def solution(mesh):
    placed = (
        P(("blk", "grp"), None),
        P(),
        P(("blk", "grp"), None),
        P(("blk", "grp")),
        P(("blk", "grp")),
        P(("blk", "grp")),
        P(),
        P(),
    )
    return jax.shard_map(
        body,
        mesh=mesh,
        in_specs=placed,
        out_specs=(P(("blk", "grp"), None), P(("blk", "grp"), None)),
        check_vma=False,
    )
```

```python
import jax
import jax.numpy as jnp
from jax import lax
from jax.experimental import pallas as pl
from jax.experimental.pallas import tpu as pltpu
from jax.sharding import PartitionSpec as P

epsilon = 1e-06
D = 1152
FEATS = 1536
ROWS = 8
TILES = D // 128
FOLD = (TILES + 1) * ROWS
MESH = pl.DeviceIdType.MESH

IMAGE_Z = ((0, -1), (1, -2), (2, -3), (3, -4))
TEXT_Z = (-4, 4, -12, 12)
IMAGE_XY = ((0, 0), (1, 0), (0, 1), (1, 1))
TEXT_XY = ((1, 1), (1, -1), (-1, 1), (-1, -1))
CHUNKS = 3
NT = (((1,), (1,)), ((), ()))
TN = (((0,), (0,)), ((), ()))


def fold(rows):
    pieces = [rows[:, 128 * t : 128 * (t + 1)] for t in range(TILES)]
    pieces.append(jnp.zeros((ROWS, 128), jnp.float32))
    return jnp.concatenate(pieces, axis=0).astype(jnp.bfloat16)


def unfold(block):
    return jnp.concatenate([block[ROWS * t : ROWS * (t + 1)] for t in range(TILES)], axis=1)


def normalize(values):
    norm_rows = jnp.sqrt(jnp.sum(values * values, axis=1, keepdims=True) + epsilon)
    return values / norm_rows, norm_rows


def column(ref, row, shift, mask):
    out = jnp.zeros((ROWS, 128), jnp.int32)
    for r in range(ROWS):
        out = jnp.where(row == r, lax.bitwise_and(lax.shift_right_logical(ref[r], shift), mask), out)
    return out


def kernel(
    scale_hbm, offset_hbm, slot_hbm, iclass_hbm, tclass_hbm, pooled_hbm, caption_hbm, w_hbm,
    image_out, text_out,
    scale_ref, offset_ref, slot_ref, iclass_ref, tclass_ref, pooled_ref, caption_ref, w_ref, wt_ref,
    own_text, img, img_s, ztxt, txt, txt_s, x_ref, mx_ref, y_ref, my_ref, tg_ref, ig_ref,
    rt1, rt1_in, rt2, rt2_in, ri1, ri1_in, ri2, ri2_in,
    load, send, recv,
):
    blk = lax.axis_index("blk")
    grp = lax.axis_index("grp")
    x, y, z, core = (blk // 4) % 4, blk % 4, (blk // 16) * 8 + grp // 2, grp % 2
    sign = 1 - 2 * core

    def device(dx=0, dy=0, dz=0, other=False):
        to_x, to_y, to_z = (x + dx + 4) % 4, (y + dy + 4) % 4, (z + dz + 32) % 32
        to_core = 1 - core if other else core
        return ((to_z // 8) * 16 + to_x * 4 + to_y, (to_z % 8) * 2 + to_core)

    partners = [dict(dz=d) for d in (-4, 4, -3, 3, -2, 2, -1, 1)]
    partners += [dict(dx=dx, dy=dy) for dx in (-1, 0, 1) for dy in (-1, 0, 1) if dx or dy]
    partners += [dict(other=True)]
    barrier = pltpu.get_barrier_semaphore()

    def greet(some):
        for p in some:
            pl.semaphore_signal(barrier, inc=1, device_id=device(**p), device_id_type=MESH)

    rows_w = FEATS // CHUNKS
    loads = [
        pltpu.make_async_copy(src, dst, load.at[n])
        for n, (src, dst) in enumerate(
            [(caption_hbm, caption_ref), (tclass_hbm, tclass_ref), (pooled_hbm, pooled_ref)]
            + [(w_hbm.at[pl.ds(rows_w * n, rows_w)], w_ref.at[pl.ds(rows_w * n, rows_w)]) for n in range(CHUNKS)]
            + [(iclass_hbm, iclass_ref), (slot_hbm, slot_ref), (scale_hbm, scale_ref), (offset_hbm, offset_ref)]
        )
    ]
    greet(partners[:4])
    for c in loads:
        c.start()
    greet(partners[4:])

    row = lax.broadcasted_iota(jnp.int32, (ROWS, 128), 0)
    lane = lax.broadcasted_iota(jnp.int32, (ROWS, 128), 1)

    def block_of(values, label):
        pieces = [values[:, 128 * t : 128 * (t + 1)] for t in range(TILES)]
        return jnp.concatenate(pieces + [label.astype(jnp.float32)], axis=0).astype(jnp.bfloat16)

    started = []

    def copy(src, dst, **to):
        n = copy.count
        copy.count += 1
        c = pltpu.make_async_remote_copy(
            src_ref=src, dst_ref=dst, send_sem=send.at[n], recv_sem=recv.at[n],
            device_id=device(**to), device_id_type=MESH,
        )
        c.start()
        started.append(c)
        return c

    copy.count = 0

    def arrive(copies):
        for c in copies:
            c.wait_recv()

    def drain():
        while started:
            started.pop(0).wait_send()

    loads[0].wait()
    loads[1].wait()
    text_dir, text_norm = normalize(caption_ref[...].astype(jnp.float32))
    label = jnp.where(lane == 0, column(tclass_ref, row, 0, 15), jnp.where(lane == 1, blk, grp * ROWS + row))
    own_text[...] = block_of(text_dir, label)
    pl.semaphore_wait(barrier, len(partners))
    near = [copy(own_text, ztxt.at[u], dz=-TEXT_Z[u]) for u in (0, 1)]

    loads[2].wait()
    embedded = jnp.zeros((ROWS, D), jnp.float32)
    for n in range(CHUNKS):
        loads[3 + n].wait()
        at = slice(rows_w * n, rows_w * (n + 1))
        embedded += jnp.dot(pooled_ref[:, at], w_ref[at, :], preferred_element_type=jnp.float32)
    image_dir, image_norm = normalize(embedded)
    for c in loads[3 + CHUNKS :]:
        c.wait()
    label = jnp.where(
        lane == 0, column(iclass_ref, row, 0, 15),
        jnp.where(lane == 1, column(slot_ref, row, 7, 63), column(slot_ref, row, 0, 127)),
    )
    img[0, 0, 0] = block_of(image_dir, label)
    along = {}
    for p in (3, 2, 1, 0):
        for i in (1, 0):
            k = IMAGE_Z[p][i]
            if k:
                along[p, i] = copy(img.at[0, 0, 0], img.at[p, 0, i], dz=-sign * k)

    def plane_text(u):
        return [copy(ztxt.at[u], txt.at[u, q], dx=-bx, dy=-by) for q, (bx, by) in enumerate(TEXT_XY)]

    plane_i, plane_t = {}, {}

    def plane_image(p):
        for i in (0, 1):
            if IMAGE_Z[p][i]:
                along[p, i].wait_recv()
        for q in (3, 2, 1):
            ax, ay = IMAGE_XY[q]
            plane_i[p, q] = copy(img.at[p, 0], img.at[p, q], dx=-sign * ax, dy=-sign * ay)

    arrive(near)
    far = [copy(ztxt.at[u], ztxt.at[2 + u], dz=-2 * TEXT_Z[u]) for u in (0, 1)]
    plane_t[0] = plane_text(0)
    plane_t[1] = plane_text(1)
    for p in range(4):
        plane_image(p)

    def spread(pair, dst, label, at):
        a, b = pair[0].astype(jnp.float32), pair[1].astype(jnp.float32)
        at = slice(at, at + 16)
        dst[at, :] = jnp.concatenate([unfold(a), unfold(b)], axis=0).astype(jnp.bfloat16)
        label[at, :] = jnp.concatenate([a[ROWS * TILES :], b[ROWS * TILES :]], axis=0).astype(jnp.bfloat16)

    cross_i, cross_t = {}, {}

    def take_image(p):
        for q in (1, 2, 3):
            plane_i[p, q].wait_recv()
        cross_i[p] = copy(img.at[p], img_s.at[p], other=True)
        for q in range(4):
            spread(img.at[p, q], x_ref, mx_ref, 64 * p + 16 * q)

    def take_text(u):
        arrive(plane_t[u])
        cross_t[u] = copy(txt.at[u], txt_s.at[u], other=True)
        for m in (0, 1):
            spread(txt.at[u, pl.ds(2 * m, 2)], y_ref, my_ref, 32 * u + 16 * m)

    def take_text_cross(u):
        cross_t[u].wait_recv()
        for m in (0, 1):
            spread(txt_s.at[u, pl.ds(2 * m, 2)], y_ref, my_ref, 128 + 32 * u + 16 * m)

    take_image(0)
    take_image(1)
    for u in (2, 3):
        far[u - 2].wait_recv()
        plane_t[u] = plane_text(u)
    take_text(0)
    take_text(1)
    take_image(2)
    take_image(3)
    take_text(2)
    take_text(3)

    scale, offset = scale_ref[0], offset_ref[0]
    basis = jnp.where(
        row == 0, jnp.where(lane == 0, 1.0, 0.0),
        jnp.where(row == 1, jnp.where(lane == 1, 128.0, jnp.where(lane == 2, 1.0, 0.0)), 0.0),
    ).astype(jnp.bfloat16)
    def weights(texts, images):
        scores = lax.dot_general(y_ref[texts, :], x_ref[images, :], NT, preferred_element_type=jnp.float32)
        scores = scores * scale + offset
        text_columns = lax.dot_general(my_ref[texts, :], basis, NT, preferred_element_type=jnp.float32)
        image_rows = lax.dot_general(basis, mx_ref[images, :], NT, preferred_element_type=jnp.float32)
        positive = text_columns[:, 1:2] == image_rows[1:2, :]
        same = text_columns[:, 0:1] == image_rows[0:1, :]
        sigmoid = 1.0 / (1.0 + jnp.exp(jnp.where(positive, scores, -scores)))
        signed = jnp.where(positive, -scale, jnp.where(same, 0.0, scale))
        return (sigmoid * signed).astype(jnp.bfloat16)

    def home_text(u):
        arrive(back_t[u])
        total = rt1_in[u, 0].astype(jnp.float32)
        for q in (1, 2, 3):
            total += rt1_in[u, q].astype(jnp.float32)
        rt2[u] = total.astype(jnp.bfloat16)
        return copy(rt2.at[u], rt2_in.at[u], dz=TEXT_Z[u])

    back_t, home_t = {}, {}
    own, other = slice(0, 128), slice(128, 256)
    weight = weights(own, slice(0, 256))
    tg_ref[...] = jnp.dot(weight, x_ref[0:256, :], preferred_element_type=jnp.float32)
    ig_ref[...] = lax.dot_general(weight, y_ref[own, :], TN, preferred_element_type=jnp.float32)
    for p in range(4):
        cross_i[p].wait_recv()
        for q in range(4):
            spread(img_s.at[p, q], x_ref, mx_ref, 256 + 64 * p + 16 * q)
    weight = weights(own, slice(256, 512))
    tg_ref[...] += jnp.dot(weight, x_ref[256:512, :], preferred_element_type=jnp.float32)
    for u in (2, 3, 0, 1):
        back_t[u] = []
        for q, (bx, by) in enumerate(TEXT_XY):
            n = 32 * u + 8 * q
            rt1[u, q] = fold(tg_ref[n : n + 8, :])
            back_t[u].append(copy(rt1.at[u, q], rt1_in.at[u, q], dx=bx, dy=by))
    for u in range(4):
        take_text_cross(u)
    weight = weights(other, slice(0, 256))
    ig_ref[...] += lax.dot_general(weight, y_ref[other, :], TN, preferred_element_type=jnp.float32)
    back_i = {}
    for p in (3, 2, 1, 0):
        for q in (3, 2, 1, 0):
            ax, ay = IMAGE_XY[q]
            for i in (0, 1):
                n = 64 * p + 16 * q + 8 * i
                ri1[p, q, i] = fold(ig_ref[n : n + 8, :])
            if q:
                back_i[p, q] = copy(ri1.at[p, q], ri1_in.at[p, q], dx=sign * ax, dy=sign * ay)

    home_i = []

    def home_image(p):
        for q in (3, 2, 1):
            back_i[p, q].wait_recv()
        for i in (1, 0):
            total = ri1[p, 0, i].astype(jnp.float32)
            for q in (1, 2, 3):
                total += ri1_in[p, q, i].astype(jnp.float32)
            ri2[p, i] = total.astype(jnp.bfloat16)
            if IMAGE_Z[p][i]:
                home_i.append(copy(ri2.at[p, i], ri2_in.at[p, i], dz=sign * IMAGE_Z[p][i]))

    home_t[2] = home_text(2)
    home_t[3] = home_text(3)
    for n in range(FEATS // 128):
        at = slice(128 * n, 128 * n + 128)
        wt_ref[:, at] = w_ref[at, :].T
    for p in (3, 2, 1, 0):
        home_image(p)
    home_t[0] = home_text(0)
    home_t[1] = home_text(1)
    drain()

    arrive(home_i)
    total = ri2[0, 0].astype(jnp.float32)
    for p in range(4):
        for i in (0, 1):
            if IMAGE_Z[p][i]:
                total += ri2_in[p, i].astype(jnp.float32)
    grad = unfold(total)
    inner = jnp.sum(image_dir * grad, axis=1, keepdims=True)
    embed_grad = ((grad - image_dir * inner) / image_norm).astype(jnp.bfloat16)
    image_out[...] = jnp.dot(embed_grad, wt_ref[...], preferred_element_type=jnp.float32).astype(jnp.bfloat16)
    arrive([home_t[u] for u in range(4)])
    total = rt2_in[0].astype(jnp.float32)
    for u in (1, 2, 3):
        total += rt2_in[u].astype(jnp.float32)
    grad = unfold(total)
    inner = jnp.sum(text_dir * grad, axis=1, keepdims=True)
    text_out[...] = ((grad - text_dir * inner) / text_norm).astype(jnp.bfloat16)


def body(
    pooled_picture_vectors,
    picture_mapping_matrix,
    caption_vectors,
    matching_caption_slot,
    picture_instance_class,
    caption_instance_class,
    score_scale,
    score_offset,
):
    vmem = pl.BlockSpec(memory_space=pltpu.VMEM)
    hbm = pl.BlockSpec(memory_space=pltpu.HBM)
    half = jnp.bfloat16
    block = (FOLD, 128)
    return pl.pallas_call(
        kernel,
        out_shape=(
            pltpu.VMEM((ROWS, FEATS), half),
            pltpu.VMEM((ROWS, D), half),
        ),
        in_specs=[hbm] * 8,
        out_specs=(vmem, vmem),
        scratch_shapes=[
            pltpu.SMEM((1,), jnp.float32),
            pltpu.SMEM((1,), jnp.float32),
            pltpu.SMEM((ROWS,), jnp.int32),
            pltpu.SMEM((ROWS,), jnp.int32),
            pltpu.SMEM((ROWS,), jnp.int32),
            pltpu.VMEM((ROWS, FEATS), half),
            pltpu.VMEM((ROWS, D), half),
            pltpu.VMEM((FEATS, D), half),
            pltpu.VMEM((D, FEATS), half),
            pltpu.VMEM(block, half),
            pltpu.VMEM((4, 4, 2) + block, half),
            pltpu.VMEM((4, 4, 2) + block, half),
            pltpu.VMEM((4,) + block, half),
            pltpu.VMEM((4, 4) + block, half),
            pltpu.VMEM((4, 4) + block, half),
            pltpu.VMEM((512, D), half),
            pltpu.VMEM((512, 128), half),
            pltpu.VMEM((256, D), half),
            pltpu.VMEM((256, 128), half),
            pltpu.VMEM((128, D), jnp.float32),
            pltpu.VMEM((256, D), jnp.float32),
            pltpu.VMEM((4, 4) + block, half),
            pltpu.VMEM((4, 4) + block, half),
            pltpu.VMEM((4,) + block, half),
            pltpu.VMEM((4,) + block, half),
            pltpu.VMEM((4, 4, 2) + block, half),
            pltpu.VMEM((4, 4, 2) + block, half),
            pltpu.VMEM((4, 2) + block, half),
            pltpu.VMEM((4, 2) + block, half),
            pltpu.SemaphoreType.DMA((10,)),
            pltpu.SemaphoreType.DMA((96,)),
            pltpu.SemaphoreType.DMA((96,)),
        ],
        compiler_params=pltpu.CompilerParams(
            collective_id=0, has_side_effects=True, vmem_limit_bytes=60 * 2**20
        ),
        name="contrast",
    )(
        score_scale, score_offset, matching_caption_slot, picture_instance_class, caption_instance_class,
        pooled_picture_vectors, caption_vectors, picture_mapping_matrix,
    )


def solution(mesh):
    placed = (
        P(("blk", "grp"), None),
        P(),
        P(("blk", "grp"), None),
        P(("blk", "grp")),
        P(("blk", "grp")),
        P(("blk", "grp")),
        P(),
        P(),
    )
    return jax.shard_map(
        body,
        mesh=mesh,
        in_specs=placed,
        out_specs=(P(("blk", "grp"), None), P(("blk", "grp"), None)),
        check_vma=False,
    )
```

```python
import jax
import jax.numpy as jnp
from jax import lax
from jax.experimental import pallas as pl
from jax.experimental.pallas import tpu as pltpu
from jax.sharding import PartitionSpec as P

epsilon = 1e-06
D = 1152
FEATS = 1536
ROWS = 8
TILES = D // 128
FOLD = (TILES + 1) * ROWS
MESH = pl.DeviceIdType.MESH

IMAGE_Z = ((0, -1), (1, -2), (2, -3), (3, -4))
TEXT_Z = (-4, 4, -12, 12)
IMAGE_XY = ((0, 0), (1, 0), (0, 1), (1, 1))
TEXT_XY = ((1, 1), (1, -1), (-1, 1), (-1, -1))
CHUNKS = 3
NT = (((1,), (1,)), ((), ()))
TN = (((0,), (0,)), ((), ()))


def fold(rows):
    pieces = [rows[:, 128 * t : 128 * (t + 1)] for t in range(TILES)]
    pieces.append(jnp.zeros((ROWS, 128), jnp.float32))
    return jnp.concatenate(pieces, axis=0).astype(jnp.bfloat16)


def unfold(block):
    return jnp.concatenate([block[ROWS * t : ROWS * (t + 1)] for t in range(TILES)], axis=1)


def normalize(values):
    norm_rows = jnp.sqrt(jnp.sum(values * values, axis=1, keepdims=True) + epsilon)
    return values / norm_rows, norm_rows


def column(ref, row, shift, mask):
    out = jnp.zeros((ROWS, 128), jnp.int32)
    for r in range(ROWS):
        out = jnp.where(row == r, lax.bitwise_and(lax.shift_right_logical(ref[r], shift), mask), out)
    return out


def kernel(
    scale_hbm, offset_hbm, slot_hbm, iclass_hbm, tclass_hbm, pooled_hbm, caption_hbm, w_hbm,
    image_out, text_out,
    scale_ref, offset_ref, slot_ref, iclass_ref, tclass_ref, pooled_ref, caption_ref, w_ref, wt_ref,
    own_text, img, img_s, ztxt, txt, txt_s, x_ref, mx_ref, y_ref, my_ref, tg_ref, ig_ref,
    rt1, rt1_in, rt2, rt2_in, ri1, ri1_in, ri2, ri2_in,
    load, send, recv,
):
    blk = lax.axis_index("blk")
    grp = lax.axis_index("grp")
    x, y, z, core = (blk // 4) % 4, blk % 4, (blk // 16) * 8 + grp // 2, grp % 2
    sign = 1 - 2 * core
    turn = -sign

    def device(dx=0, dy=0, dz=0, other=False):
        to_x, to_y, to_z = (x + dx + 4) % 4, (y + dy + 4) % 4, (z + dz + 32) % 32
        to_core = 1 - core if other else core
        return ((to_z // 8) * 16 + to_x * 4 + to_y, (to_z % 8) * 2 + to_core)

    partners = [dict(dz=d) for d in (-4, 4, -3, 3, -2, 2, -1, 1)]
    partners += [dict(dx=dx, dy=dy) for dx in (-1, 0, 1) for dy in (-1, 0, 1) if dx or dy]
    partners += [dict(other=True)]
    barrier = pltpu.get_barrier_semaphore()

    def greet(some):
        for p in some:
            pl.semaphore_signal(barrier, inc=1, device_id=device(**p), device_id_type=MESH)

    rows_w = FEATS // CHUNKS
    loads = [
        pltpu.make_async_copy(src, dst, load.at[n])
        for n, (src, dst) in enumerate(
            [(caption_hbm, caption_ref), (tclass_hbm, tclass_ref), (pooled_hbm, pooled_ref)]
            + [(w_hbm.at[pl.ds(rows_w * n, rows_w)], w_ref.at[pl.ds(rows_w * n, rows_w)]) for n in range(CHUNKS)]
            + [(iclass_hbm, iclass_ref), (slot_hbm, slot_ref), (scale_hbm, scale_ref), (offset_hbm, offset_ref)]
        )
    ]
    greet(partners[:4])
    for c in loads:
        c.start()
    greet(partners[4:])

    row = lax.broadcasted_iota(jnp.int32, (ROWS, 128), 0)
    lane = lax.broadcasted_iota(jnp.int32, (ROWS, 128), 1)

    def block_of(values, label):
        pieces = [values[:, 128 * t : 128 * (t + 1)] for t in range(TILES)]
        return jnp.concatenate(pieces + [label.astype(jnp.float32)], axis=0).astype(jnp.bfloat16)

    started = []

    def copy(src, dst, n=None, **to):
        if n is None:
            n = copy.count
            copy.count += 1
        c = pltpu.make_async_remote_copy(
            src_ref=src, dst_ref=dst, send_sem=send.at[n], recv_sem=recv.at[n],
            device_id=device(**to), device_id_type=MESH,
        )
        c.start()
        started.append(c)
        return c

    copy.count = 0

    def arrive(copies):
        for c in copies:
            c.wait_recv()

    def drain():
        while started:
            started.pop(0).wait_send()

    loads[0].wait()
    loads[1].wait()
    text_dir, text_norm = normalize(caption_ref[...].astype(jnp.float32))
    label = jnp.where(lane == 0, column(tclass_ref, row, 0, 15), jnp.where(lane == 1, blk, grp * ROWS + row))
    own_text[...] = block_of(text_dir, label)
    pl.semaphore_wait(barrier, len(partners))
    near = [copy(own_text, ztxt.at[u], dz=-TEXT_Z[u]) for u in (0, 1)]

    loads[2].wait()
    embedded = jnp.zeros((ROWS, D), jnp.float32)
    for n in range(CHUNKS):
        loads[3 + n].wait()
        at = slice(rows_w * n, rows_w * (n + 1))
        embedded += jnp.dot(pooled_ref[:, at], w_ref[at, :], preferred_element_type=jnp.float32)
    image_dir, image_norm = normalize(embedded)
    for c in loads[3 + CHUNKS :]:
        c.wait()
    label = jnp.where(
        lane == 0, column(iclass_ref, row, 0, 15),
        jnp.where(lane == 1, column(slot_ref, row, 7, 63), column(slot_ref, row, 0, 127)),
    )
    img[0, 0, 0] = block_of(image_dir, label)
    along = {}
    for p in (3, 2, 1, 0):
        for i in (1, 0):
            k = IMAGE_Z[p][i]
            if k:
                along[p, i] = copy(img.at[0, 0, 0], img.at[p, 0, i], dz=-sign * k)

    def plane_text(u):
        return [copy(ztxt.at[u], txt.at[u, q], dx=-bx, dy=-by) for q, (bx, by) in enumerate(TEXT_XY)]

    plane_i, plane_t = {}, {}

    def plane_image(p):
        for i in (0, 1):
            if IMAGE_Z[p][i]:
                along[p, i].wait_recv()
        for q in (3, 2, 1):
            ax, ay = IMAGE_XY[q]
            plane_i[p, q] = copy(img.at[p, 0], img.at[p, q], dx=-turn * ax, dy=-turn * ay)

    arrive(near)
    far = [copy(ztxt.at[u], ztxt.at[2 + u], dz=-2 * TEXT_Z[u]) for u in (0, 1)]
    plane_t[0] = plane_text(0)
    plane_t[1] = plane_text(1)
    for p in range(4):
        plane_image(p)

    def spread(pair, dst, label, at):
        a, b = pair[0].astype(jnp.float32), pair[1].astype(jnp.float32)
        at = slice(at, at + 16)
        dst[at, :] = jnp.concatenate([unfold(a), unfold(b)], axis=0).astype(jnp.bfloat16)
        label[at, :] = jnp.concatenate([a[ROWS * TILES :], b[ROWS * TILES :]], axis=0).astype(jnp.bfloat16)

    cross_i, cross_t = {}, {}

    def take_image(p):
        for q in (1, 2, 3):
            plane_i[p, q].wait_recv()
        cross_i[p] = copy(img.at[p], img_s.at[p], other=True)
        for q in range(4):
            spread(img.at[p, q], x_ref, mx_ref, 64 * p + 16 * q)

    def take_text(u):
        arrive(plane_t[u])
        cross_t[u] = copy(txt.at[u], txt_s.at[u], other=True)
        for m in (0, 1):
            spread(txt.at[u, pl.ds(2 * m, 2)], y_ref, my_ref, 32 * u + 16 * m)

    def take_text_cross(u):
        cross_t[u].wait_recv()
        for m in (0, 1):
            spread(txt_s.at[u, pl.ds(2 * m, 2)], y_ref, my_ref, 128 + 32 * u + 16 * m)

    take_image(0)
    take_image(1)
    for u in (2, 3):
        far[u - 2].wait_recv()
        plane_t[u] = plane_text(u)
    take_text(0)
    take_text(1)
    take_image(2)
    take_image(3)
    take_text(2)
    take_text(3)

    scale, offset = scale_ref[0], offset_ref[0]
    basis = jnp.where(
        row == 0, jnp.where(lane == 0, 1.0, 0.0),
        jnp.where(row == 1, jnp.where(lane == 1, 128.0, jnp.where(lane == 2, 1.0, 0.0)), 0.0),
    ).astype(jnp.bfloat16)
    def weights(texts, images):
        scores = lax.dot_general(y_ref[texts, :], x_ref[images, :], NT, preferred_element_type=jnp.float32)
        scores = scores * scale + offset
        text_columns = lax.dot_general(my_ref[texts, :], basis, NT, preferred_element_type=jnp.float32)
        image_rows = lax.dot_general(basis, mx_ref[images, :], NT, preferred_element_type=jnp.float32)
        positive = text_columns[:, 1:2] == image_rows[1:2, :]
        same = text_columns[:, 0:1] == image_rows[0:1, :]
        sigmoid = 1.0 / (1.0 + jnp.exp(jnp.where(positive, scores, -scores)))
        signed = jnp.where(positive, -scale, jnp.where(same, 0.0, scale))
        return (sigmoid * signed).astype(jnp.bfloat16)

    far_first = ((z + 4) // 16) % 2
    ahead, behind = 2 * far_first, 2 - 2 * far_first

    def plane_back(u):
        out = []
        for q, (bx, by) in enumerate(TEXT_XY):
            n = pl.multiple_of(32 * u + 8 * q, 8)
            rt1[u, q] = fold(tg_ref[pl.ds(n, 8), :])
            out.append(copy(rt1.at[u, q], rt1_in.at[u, q], n=80 + 4 * u + q, dx=bx, dy=by))
        return out

    def home_text(u, arriving):
        arrive(arriving)
        total = rt1_in[u, 0].astype(jnp.float32)
        for q in (1, 2, 3):
            total += rt1_in[u, q].astype(jnp.float32)
        rt2[u] = total.astype(jnp.bfloat16)
        return copy(rt2.at[u], rt2_in.at[u], n=96 + u, dz=(2 * (u % 2) - 1) * (4 + 8 * (u // 2)))

    home_t = []
    own, other = slice(0, 128), slice(128, 256)
    weight = weights(own, slice(0, 256))
    tg_ref[...] = jnp.dot(weight, x_ref[0:256, :], preferred_element_type=jnp.float32)
    ig_ref[...] = lax.dot_general(weight, y_ref[own, :], TN, preferred_element_type=jnp.float32)
    for p in range(4):
        cross_i[p].wait_recv()
        for q in range(4):
            spread(img_s.at[p, q], x_ref, mx_ref, 256 + 64 * p + 16 * q)
    weight = weights(own, slice(256, 512))
    tg_ref[...] += jnp.dot(weight, x_ref[256:512, :], preferred_element_type=jnp.float32)
    back_ahead = [plane_back(ahead + i) for i in (0, 1)]
    for u in range(4):
        take_text_cross(u)
    weight = weights(other, slice(0, 256))
    ig_ref[...] += lax.dot_general(weight, y_ref[other, :], TN, preferred_element_type=jnp.float32)
    back_i = {}
    for p in (3, 2, 1, 0):
        for q in (3, 2, 1, 0):
            ax, ay = IMAGE_XY[q]
            n = 64 * p + 16 * q
            pieces = [ig_ref[n : n + 16, 128 * t : 128 * (t + 1)] for t in range(TILES)]
            ri1[p, q] = jnp.concatenate(pieces, axis=0).astype(jnp.bfloat16)
            if q:
                back_i[p, q] = copy(ri1.at[p, q], ri1_in.at[p, q], dx=turn * ax, dy=turn * ay)

    back_behind = [plane_back(behind + i) for i in (0, 1)]
    home_i = []

    def home_image(p):
        for q in (3, 2, 1):
            back_i[p, q].wait_recv()
        total = ri1[p, 0].astype(jnp.float32)
        for q in (1, 2, 3):
            total += ri1_in[p, q].astype(jnp.float32)
        for i in (1, 0):
            pieces = [total[16 * t + 8 * i : 16 * t + 8 * i + 8] for t in range(TILES)]
            pieces.append(jnp.zeros((ROWS, 128), jnp.float32))
            ri2[p, i] = jnp.concatenate(pieces, axis=0).astype(jnp.bfloat16)
            if IMAGE_Z[p][i]:
                home_i.append(copy(ri2.at[p, i], ri2_in.at[p, i], dz=sign * IMAGE_Z[p][i]))

    home_t += [home_text(ahead + i, back_ahead[i]) for i in (0, 1)]
    for n in range(FEATS // 128):
        at = slice(128 * n, 128 * n + 128)
        wt_ref[:, at] = w_ref[at, :].T
    for p in (3, 2, 1, 0):
        home_image(p)
    home_t += [home_text(behind + i, back_behind[i]) for i in (0, 1)]
    drain()

    arrive(home_i)
    total = ri2[0, 0].astype(jnp.float32)
    for p in range(4):
        for i in (0, 1):
            if IMAGE_Z[p][i]:
                total += ri2_in[p, i].astype(jnp.float32)
    grad = unfold(total)
    inner = jnp.sum(image_dir * grad, axis=1, keepdims=True)
    embed_grad = ((grad - image_dir * inner) / image_norm).astype(jnp.bfloat16)
    image_out[...] = jnp.dot(embed_grad, wt_ref[...], preferred_element_type=jnp.float32).astype(jnp.bfloat16)
    arrive(home_t)
    total = rt2_in[0].astype(jnp.float32)
    for u in (1, 2, 3):
        total += rt2_in[u].astype(jnp.float32)
    grad = unfold(total)
    inner = jnp.sum(text_dir * grad, axis=1, keepdims=True)
    text_out[...] = ((grad - text_dir * inner) / text_norm).astype(jnp.bfloat16)


def body(
    pooled_picture_vectors,
    picture_mapping_matrix,
    caption_vectors,
    matching_caption_slot,
    picture_instance_class,
    caption_instance_class,
    score_scale,
    score_offset,
):
    vmem = pl.BlockSpec(memory_space=pltpu.VMEM)
    hbm = pl.BlockSpec(memory_space=pltpu.HBM)
    half = jnp.bfloat16
    block = (FOLD, 128)
    return pl.pallas_call(
        kernel,
        out_shape=(
            pltpu.VMEM((ROWS, FEATS), half),
            pltpu.VMEM((ROWS, D), half),
        ),
        in_specs=[hbm] * 8,
        out_specs=(vmem, vmem),
        scratch_shapes=[
            pltpu.SMEM((1,), jnp.float32),
            pltpu.SMEM((1,), jnp.float32),
            pltpu.SMEM((ROWS,), jnp.int32),
            pltpu.SMEM((ROWS,), jnp.int32),
            pltpu.SMEM((ROWS,), jnp.int32),
            pltpu.VMEM((ROWS, FEATS), half),
            pltpu.VMEM((ROWS, D), half),
            pltpu.VMEM((FEATS, D), half),
            pltpu.VMEM((D, FEATS), half),
            pltpu.VMEM(block, half),
            pltpu.VMEM((4, 4, 2) + block, half),
            pltpu.VMEM((4, 4, 2) + block, half),
            pltpu.VMEM((4,) + block, half),
            pltpu.VMEM((4, 4) + block, half),
            pltpu.VMEM((4, 4) + block, half),
            pltpu.VMEM((512, D), half),
            pltpu.VMEM((512, 128), half),
            pltpu.VMEM((256, D), half),
            pltpu.VMEM((256, 128), half),
            pltpu.VMEM((128, D), jnp.float32),
            pltpu.VMEM((256, D), jnp.float32),
            pltpu.VMEM((4, 4) + block, half),
            pltpu.VMEM((4, 4) + block, half),
            pltpu.VMEM((4,) + block, half),
            pltpu.VMEM((4,) + block, half),
            pltpu.VMEM((4, 4, 2 * D // 16, 128), half),
            pltpu.VMEM((4, 4, 2 * D // 16, 128), half),
            pltpu.VMEM((4, 2) + block, half),
            pltpu.VMEM((4, 2) + block, half),
            pltpu.SemaphoreType.DMA((10,)),
            pltpu.SemaphoreType.DMA((100,)),
            pltpu.SemaphoreType.DMA((100,)),
        ],
        compiler_params=pltpu.CompilerParams(
            collective_id=0, has_side_effects=True, vmem_limit_bytes=60 * 2**20
        ),
        name="contrast",
    )(
        score_scale, score_offset, matching_caption_slot, picture_instance_class, caption_instance_class,
        pooled_picture_vectors, caption_vectors, picture_mapping_matrix,
    )


def solution(mesh):
    placed = (
        P(("blk", "grp"), None),
        P(),
        P(("blk", "grp"), None),
        P(("blk", "grp")),
        P(("blk", "grp")),
        P(("blk", "grp")),
        P(),
        P(),
    )
    return jax.shard_map(
        body,
        mesh=mesh,
        in_specs=placed,
        out_specs=(P(("blk", "grp"), None), P(("blk", "grp"), None)),
        check_vma=False,
    )
```

```python
import jax
import jax.numpy as jnp
from jax import lax
from jax.experimental import pallas as pl
from jax.experimental.pallas import tpu as pltpu
from jax.sharding import PartitionSpec as P

epsilon = 1e-06
D = 1152
FEATS = 1536
ROWS = 8
TILES = D // 128
FOLD = (TILES + 1) * ROWS
MESH = pl.DeviceIdType.MESH

IMAGE_Z = ((0, -1), (1, -2), (2, -3), (3, -4))
TEXT_Z = (-4, 4, -12, 12)
IMAGE_XY = ((0, 0), (1, 0), (0, 1), (1, 1))
TEXT_XY = ((1, 1), (-1, -1), (1, -1), (-1, 1))
CHUNKS = 3
NT = (((1,), (1,)), ((), ()))
TN = (((0,), (0,)), ((), ()))


def fold(rows):
    pieces = [rows[:, 128 * t : 128 * (t + 1)] for t in range(TILES)]
    pieces.append(jnp.zeros((ROWS, 128), jnp.float32))
    return jnp.concatenate(pieces, axis=0).astype(jnp.bfloat16)


def unfold(block):
    return jnp.concatenate([block[ROWS * t : ROWS * (t + 1)] for t in range(TILES)], axis=1)


def normalize(values):
    norm_rows = jnp.sqrt(jnp.sum(values * values, axis=1, keepdims=True) + epsilon)
    return values / norm_rows, norm_rows


def column(ref, row, shift, mask):
    out = jnp.zeros((ROWS, 128), jnp.int32)
    for r in range(ROWS):
        out = jnp.where(row == r, lax.bitwise_and(lax.shift_right_logical(ref[r], shift), mask), out)
    return out


def kernel(
    scale_hbm, offset_hbm, slot_hbm, iclass_hbm, tclass_hbm, pooled_hbm, caption_hbm, w_hbm,
    image_out, text_out,
    scale_ref, offset_ref, slot_ref, iclass_ref, tclass_ref, pooled_ref, caption_ref, w_ref, wt_ref,
    own_text, img, img_s, ztxt, txt, txt_s, x_ref, mx_ref, y_ref, my_ref, tg_ref, ig_ref,
    rt1, rt1_in, rt2, rt2_in, ri1, ri1_in, ri2, ri2_in,
    load, send, recv,
):
    blk = lax.axis_index("blk")
    grp = lax.axis_index("grp")
    x, y, z, core = (blk // 4) % 4, blk % 4, (blk // 16) * 8 + grp // 2, grp % 2
    sign = 1 - 2 * core
    turn = -sign

    def device(dx=0, dy=0, dz=0, other=False):
        to_x, to_y, to_z = (x + dx + 4) % 4, (y + dy + 4) % 4, (z + dz + 32) % 32
        to_core = 1 - core if other else core
        return ((to_z // 8) * 16 + to_x * 4 + to_y, (to_z % 8) * 2 + to_core)

    partners = [dict(dz=d) for d in (-4, 4, -3, 3, -2, 2, -1, 1)]
    partners += [dict(dx=dx, dy=dy) for dx in (-1, 0, 1) for dy in (-1, 0, 1) if dx or dy]
    partners += [dict(other=True)]
    barrier = pltpu.get_barrier_semaphore()

    def greet(some):
        for p in some:
            pl.semaphore_signal(barrier, inc=1, device_id=device(**p), device_id_type=MESH)

    rows_w = FEATS // CHUNKS
    loads = [
        pltpu.make_async_copy(src, dst, load.at[n])
        for n, (src, dst) in enumerate(
            [(caption_hbm, caption_ref), (tclass_hbm, tclass_ref), (pooled_hbm, pooled_ref)]
            + [(w_hbm.at[pl.ds(rows_w * n, rows_w)], w_ref.at[pl.ds(rows_w * n, rows_w)]) for n in range(CHUNKS)]
            + [(iclass_hbm, iclass_ref), (slot_hbm, slot_ref), (scale_hbm, scale_ref), (offset_hbm, offset_ref)]
        )
    ]
    greet(partners[:4])
    for c in loads:
        c.start()
    greet(partners[4:])

    row = lax.broadcasted_iota(jnp.int32, (ROWS, 128), 0)
    lane = lax.broadcasted_iota(jnp.int32, (ROWS, 128), 1)

    def block_of(values, label):
        pieces = [values[:, 128 * t : 128 * (t + 1)] for t in range(TILES)]
        return jnp.concatenate(pieces + [label.astype(jnp.float32)], axis=0).astype(jnp.bfloat16)

    started = []

    def copy(src, dst, n=None, **to):
        if n is None:
            n = copy.count
            copy.count += 1
        c = pltpu.make_async_remote_copy(
            src_ref=src, dst_ref=dst, send_sem=send.at[n], recv_sem=recv.at[n],
            device_id=device(**to), device_id_type=MESH,
        )
        c.start()
        started.append(c)
        return c

    copy.count = 0

    def arrive(copies):
        for c in copies:
            c.wait_recv()

    def drain():
        while started:
            started.pop(0).wait_send()

    loads[0].wait()
    loads[1].wait()
    text_dir, text_norm = normalize(caption_ref[...].astype(jnp.float32))
    label = jnp.where(lane == 0, column(tclass_ref, row, 0, 15), jnp.where(lane == 1, blk, grp * ROWS + row))
    own_text[...] = block_of(text_dir, label)
    pl.semaphore_wait(barrier, len(partners))
    near = [copy(own_text, ztxt.at[u], dz=-TEXT_Z[u]) for u in (0, 1)]

    loads[2].wait()
    embedded = jnp.zeros((ROWS, D), jnp.float32)
    for n in range(CHUNKS):
        loads[3 + n].wait()
        at = slice(rows_w * n, rows_w * (n + 1))
        embedded += jnp.dot(pooled_ref[:, at], w_ref[at, :], preferred_element_type=jnp.float32)
    image_dir, image_norm = normalize(embedded)
    for c in loads[3 + CHUNKS :]:
        c.wait()
    label = jnp.where(
        lane == 0, column(iclass_ref, row, 0, 15),
        jnp.where(lane == 1, column(slot_ref, row, 7, 63), column(slot_ref, row, 0, 127)),
    )
    img[0, 0, 0] = block_of(image_dir, label)
    along = {}
    for p in (3, 2, 1, 0):
        for i in (1, 0):
            k = IMAGE_Z[p][i]
            if k:
                along[p, i] = copy(img.at[0, 0, 0], img.at[p, 0, i], dz=-sign * k)

    def plane_text(u):
        return [copy(ztxt.at[u], txt.at[u, q], dx=-turn * bx, dy=-turn * by) for q, (bx, by) in enumerate(TEXT_XY)]

    plane_i, plane_t = {}, {}

    def plane_image(p):
        for i in (0, 1):
            if IMAGE_Z[p][i]:
                along[p, i].wait_recv()
        for q in (3, 2, 1):
            ax, ay = IMAGE_XY[q]
            plane_i[p, q] = copy(img.at[p, 0], img.at[p, q], dx=-turn * ax, dy=-turn * ay)

    arrive(near)
    far = [copy(ztxt.at[u], ztxt.at[2 + u], dz=-2 * TEXT_Z[u]) for u in (0, 1)]
    plane_t[0] = plane_text(0)
    plane_t[1] = plane_text(1)
    for p in range(4):
        plane_image(p)

    def spread(pair, dst, label, at):
        a, b = pair[0].astype(jnp.float32), pair[1].astype(jnp.float32)
        at = slice(at, at + 16)
        dst[at, :] = jnp.concatenate([unfold(a), unfold(b)], axis=0).astype(jnp.bfloat16)
        label[at, :] = jnp.concatenate([a[ROWS * TILES :], b[ROWS * TILES :]], axis=0).astype(jnp.bfloat16)

    cross_i, cross_t = {}, {}

    def take_image(p):
        for q in (1, 2, 3):
            plane_i[p, q].wait_recv()
        cross_i[p] = copy(img.at[p], img_s.at[p], other=True)
        for q in range(4):
            spread(img.at[p, q], x_ref, mx_ref, 64 * p + 16 * q)

    def take_text(u):
        arrive(plane_t[u])
        cross_t[u] = copy(txt.at[u], txt_s.at[u], other=True)
        for m in (0, 1):
            spread(txt.at[u, pl.ds(2 * m, 2)], y_ref, my_ref, 32 * u + 16 * m)

    def take_text_cross(u):
        cross_t[u].wait_recv()
        for m in (0, 1):
            spread(txt_s.at[u, pl.ds(2 * m, 2)], y_ref, my_ref, 128 + 32 * u + 16 * m)

    take_image(0)
    take_image(1)
    for u in (2, 3):
        far[u - 2].wait_recv()
        plane_t[u] = plane_text(u)
    take_text(0)
    take_text(1)
    take_image(2)
    take_image(3)
    take_text(2)
    take_text(3)

    scale, offset = scale_ref[0], offset_ref[0]
    basis = jnp.where(
        row == 0, jnp.where(lane == 0, 1.0, 0.0),
        jnp.where(row == 1, jnp.where(lane == 1, 128.0, jnp.where(lane == 2, 1.0, 0.0)), 0.0),
    ).astype(jnp.bfloat16)
    def weights(texts, images):
        scores = lax.dot_general(y_ref[texts, :], x_ref[images, :], NT, preferred_element_type=jnp.float32)
        scores = scores * scale + offset
        text_columns = lax.dot_general(my_ref[texts, :], basis, NT, preferred_element_type=jnp.float32)
        image_rows = lax.dot_general(basis, mx_ref[images, :], NT, preferred_element_type=jnp.float32)
        positive = text_columns[:, 1:2] == image_rows[1:2, :]
        same = text_columns[:, 0:1] == image_rows[0:1, :]
        sigmoid = 1.0 / (1.0 + jnp.exp(jnp.where(positive, scores, -scores)))
        signed = jnp.where(positive, -scale, jnp.where(same, 0.0, scale))
        return (sigmoid * signed).astype(jnp.bfloat16)

    ahead = ((z + 4) // 16) % 2
    behind = 1 - ahead

    def plane_back(pair):
        out = []
        for q, (bx, by) in enumerate(TEXT_XY):
            n = 64 * pair + 8 * q
            both = [tg_ref[pl.ds(pl.multiple_of(n + 32 * i, 8), 8), :] for i in (0, 1)]
            rows = jnp.concatenate(both, axis=0)
            pieces = [rows[:, 128 * t : 128 * (t + 1)] for t in range(TILES)]
            rt1[pair, q] = jnp.concatenate(pieces, axis=0).astype(jnp.bfloat16)
            out.append(
                copy(rt1.at[pair, q], rt1_in.at[pair, q], n=80 + 4 * pair + q, dx=turn * bx, dy=turn * by)
            )
        return out

    def home_text(pair, arriving):
        arrive(arriving)
        total = rt1_in[pair, 0].astype(jnp.float32)
        for q in (1, 2, 3):
            total += rt1_in[pair, q].astype(jnp.float32)
        out = []
        for i in (0, 1):
            u = 2 * pair + i
            pieces = [total[16 * t + 8 * i : 16 * t + 8 * i + 8] for t in range(TILES)]
            pieces.append(jnp.zeros((ROWS, 128), jnp.float32))
            rt2[u] = jnp.concatenate(pieces, axis=0).astype(jnp.bfloat16)
            out.append(copy(rt2.at[u], rt2_in.at[u], n=96 + u, dz=(2 * i - 1) * (4 + 8 * pair)))
        return out

    home_t = []
    own, other = slice(0, 128), slice(128, 256)
    weight = weights(own, slice(0, 256))
    tg_ref[...] = jnp.dot(weight, x_ref[0:256, :], preferred_element_type=jnp.float32)
    ig_ref[...] = lax.dot_general(weight, y_ref[own, :], TN, preferred_element_type=jnp.float32)
    for p in range(4):
        cross_i[p].wait_recv()
        for q in range(4):
            spread(img_s.at[p, q], x_ref, mx_ref, 256 + 64 * p + 16 * q)
    weight = weights(own, slice(256, 512))
    tg_ref[...] += jnp.dot(weight, x_ref[256:512, :], preferred_element_type=jnp.float32)
    back_ahead = plane_back(ahead)
    for u in range(4):
        take_text_cross(u)
    weight = weights(other, slice(0, 256))
    ig_ref[...] += lax.dot_general(weight, y_ref[other, :], TN, preferred_element_type=jnp.float32)
    back_i = {}
    for p in (3, 2, 1, 0):
        for q in (3, 2, 1, 0):
            ax, ay = IMAGE_XY[q]
            n = 64 * p + 16 * q
            pieces = [ig_ref[n : n + 16, 128 * t : 128 * (t + 1)] for t in range(TILES)]
            ri1[p, q] = jnp.concatenate(pieces, axis=0).astype(jnp.bfloat16)
            if q:
                back_i[p, q] = copy(ri1.at[p, q], ri1_in.at[p, q], dx=turn * ax, dy=turn * ay)

    back_behind = plane_back(behind)
    home_i = []

    def home_image(p):
        for q in (3, 2, 1):
            back_i[p, q].wait_recv()
        total = ri1[p, 0].astype(jnp.float32)
        for q in (1, 2, 3):
            total += ri1_in[p, q].astype(jnp.float32)
        for i in (1, 0):
            pieces = [total[16 * t + 8 * i : 16 * t + 8 * i + 8] for t in range(TILES)]
            pieces.append(jnp.zeros((ROWS, 128), jnp.float32))
            ri2[p, i] = jnp.concatenate(pieces, axis=0).astype(jnp.bfloat16)
            if IMAGE_Z[p][i]:
                home_i.append(copy(ri2.at[p, i], ri2_in.at[p, i], dz=sign * IMAGE_Z[p][i]))

    home_t += home_text(ahead, back_ahead)
    for n in range(FEATS // 128):
        at = slice(128 * n, 128 * n + 128)
        wt_ref[:, at] = w_ref[at, :].T
    for p in (3, 2, 1, 0):
        home_image(p)
    home_t += home_text(behind, back_behind)
    drain()

    arrive(home_i)
    total = ri2[0, 0].astype(jnp.float32)
    for p in range(4):
        for i in (0, 1):
            if IMAGE_Z[p][i]:
                total += ri2_in[p, i].astype(jnp.float32)
    grad = unfold(total)
    inner = jnp.sum(image_dir * grad, axis=1, keepdims=True)
    embed_grad = ((grad - image_dir * inner) / image_norm).astype(jnp.bfloat16)
    image_out[...] = jnp.dot(embed_grad, wt_ref[...], preferred_element_type=jnp.float32).astype(jnp.bfloat16)
    arrive(home_t)
    total = rt2_in[0].astype(jnp.float32)
    for u in (1, 2, 3):
        total += rt2_in[u].astype(jnp.float32)
    grad = unfold(total)
    inner = jnp.sum(text_dir * grad, axis=1, keepdims=True)
    text_out[...] = ((grad - text_dir * inner) / text_norm).astype(jnp.bfloat16)


def body(
    pooled_picture_vectors,
    picture_mapping_matrix,
    caption_vectors,
    matching_caption_slot,
    picture_instance_class,
    caption_instance_class,
    score_scale,
    score_offset,
):
    vmem = pl.BlockSpec(memory_space=pltpu.VMEM)
    hbm = pl.BlockSpec(memory_space=pltpu.HBM)
    half = jnp.bfloat16
    block = (FOLD, 128)
    return pl.pallas_call(
        kernel,
        out_shape=(
            pltpu.VMEM((ROWS, FEATS), half),
            pltpu.VMEM((ROWS, D), half),
        ),
        in_specs=[hbm] * 8,
        out_specs=(vmem, vmem),
        scratch_shapes=[
            pltpu.SMEM((1,), jnp.float32),
            pltpu.SMEM((1,), jnp.float32),
            pltpu.SMEM((ROWS,), jnp.int32),
            pltpu.SMEM((ROWS,), jnp.int32),
            pltpu.SMEM((ROWS,), jnp.int32),
            pltpu.VMEM((ROWS, FEATS), half),
            pltpu.VMEM((ROWS, D), half),
            pltpu.VMEM((FEATS, D), half),
            pltpu.VMEM((D, FEATS), half),
            pltpu.VMEM(block, half),
            pltpu.VMEM((4, 4, 2) + block, half),
            pltpu.VMEM((4, 4, 2) + block, half),
            pltpu.VMEM((4,) + block, half),
            pltpu.VMEM((4, 4) + block, half),
            pltpu.VMEM((4, 4) + block, half),
            pltpu.VMEM((512, D), half),
            pltpu.VMEM((512, 128), half),
            pltpu.VMEM((256, D), half),
            pltpu.VMEM((256, 128), half),
            pltpu.VMEM((128, D), jnp.float32),
            pltpu.VMEM((256, D), jnp.float32),
            pltpu.VMEM((2, 4, 2 * D // 16, 128), half),
            pltpu.VMEM((2, 4, 2 * D // 16, 128), half),
            pltpu.VMEM((4,) + block, half),
            pltpu.VMEM((4,) + block, half),
            pltpu.VMEM((4, 4, 2 * D // 16, 128), half),
            pltpu.VMEM((4, 4, 2 * D // 16, 128), half),
            pltpu.VMEM((4, 2) + block, half),
            pltpu.VMEM((4, 2) + block, half),
            pltpu.SemaphoreType.DMA((10,)),
            pltpu.SemaphoreType.DMA((100,)),
            pltpu.SemaphoreType.DMA((100,)),
        ],
        compiler_params=pltpu.CompilerParams(
            collective_id=0, has_side_effects=True, vmem_limit_bytes=60 * 2**20
        ),
        name="contrast",
    )(
        score_scale, score_offset, matching_caption_slot, picture_instance_class, caption_instance_class,
        pooled_picture_vectors, caption_vectors, picture_mapping_matrix,
    )


def solution(mesh):
    placed = (
        P(("blk", "grp"), None),
        P(),
        P(("blk", "grp"), None),
        P(("blk", "grp")),
        P(("blk", "grp")),
        P(("blk", "grp")),
        P(),
        P(),
    )
    return jax.shard_map(
        body,
        mesh=mesh,
        in_specs=placed,
        out_specs=(P(("blk", "grp"), None), P(("blk", "grp"), None)),
        check_vma=False,
    )
```
